32 devices in a mesh: tm: 8 (over z, core), space: 4 (over y, x).
Axes of the slice: x: 2, y: 2, z: 4, core: 2. Of those that a mesh axis runs over, the one named last changes fastest.
Arguments:
- iterate: float32 [64, 4, 128, 128], P('tm', 'space'), may hold values from -6 to 6
- forcing: float32 [64, 4, 128, 128], P('tm', 'space'), may hold values from -6 to 6
- start_field: float32 [4, 128, 128], P('space'), may hold values from -6 to 6
- classes: int32 [4, 128, 128], P('space'), may hold values from 0 to 7
- open_mask: int32 [4, 128, 128], P('space'), may hold values 0 or 1
- diffusivity: float32 [8], replicated, may hold values from 0.3 to 3
- drift: float32 [3, 8], replicated, may hold values from -0.9 to 0.9
Outputs:
- residual: float32 [64, 4, 128, 128], P('tm', 'space')
- corrected: float32 [64, 4, 128, 128], P('tm', 'space')
The draws below stay inside these ranges and needn't reach their ends.
All inputs are finite; a program needn't handle non-finite values. No bound on the sum of `open_mask` on one device may be relied on, other than what follows from the above.
Results may differ from the reference program's by a relative error of at most 0.0003.
Values sent between devices are 32-bit elements; how exact they have to be, the bound alone decides.
A program may use at most 64 MiB of HBM per device.

```python
import math
import jax
import jax.numpy as jnp
from jax import lax

NY = 128
NZ = 128
SWEEPS = 4
NCLASS = 8
NX = 4
L = 64


def place_ends(result, rng, low, top_value):
    dims = result.shape
    index_at = [jax.random.randint(jax.random.fold_in(rng, axis), (), 0, dims[axis]) for axis in range(len(dims))]
    result = result.at[tuple(index_at)].set(low)
    longest = dims.index(max(dims))
    index_at[longest] = (index_at[longest] + 1) % dims[longest]
    return result.at[tuple(index_at)].set(top_value)


def block_scale(key, extent, shards, least, largest):
    factor_of, own = 1.0, jax.random.fold_in(key, 6)
    for axis_at, blocks in shards:
        heights = jnp.exp(jax.random.uniform(jax.random.fold_in(own, axis_at), (blocks,), jnp.float32, least / len(shards), largest / len(shards)))
        factor_of = factor_of * jnp.repeat(heights, extent[axis_at] // blocks).reshape([-1 if axis == axis_at else 1 for axis in range(len(extent))])
    return factor_of


def noise(key, extent, deviation, reach, shards=(), held_as=jnp.bfloat16):
    entries = deviation * jax.random.normal(key, extent, jnp.float32)
    if shards:
        entries = entries * block_scale(key, extent, shards, -0.22, 0.18)
    return jnp.clip(entries, -reach, reach).astype(held_as)


def setup_inputs(seed: int = 0) -> dict:
    key_of = jax.random.split(jax.random.key(seed), 8)
    iterate = noise(key_of[0], (L, NX, NY, NZ), 1.0, 6.0, ((0, 8), (1, 4)), jnp.float32)
    forcing = noise(key_of[1], (L, NX, NY, NZ), 1.0, 6.0, ((0, 8), (1, 4)), jnp.float32)
    start_field = noise(key_of[2], (NX, NY, NZ), 1.0, 6.0, ((0, 4),), jnp.float32)
    classes = place_ends(jax.random.randint(key_of[3], (NX, NY, NZ), 0, NCLASS), jax.random.fold_in(key_of[3], 1), 0, NCLASS - 1).astype(jnp.int32)
    open_mask = place_ends((jax.random.randint(key_of[4], (NX, NY, NZ), 0, 8) < 7).astype(jnp.int32), jax.random.fold_in(key_of[4], 1), 0, 1)
    diffusivity = jnp.clip(jnp.exp(jax.random.uniform(key_of[5], (NCLASS,), jnp.float32, math.log(0.3), math.log(3.0))), 0.3, 3.0)
    drift = jnp.clip(jax.random.uniform(key_of[6], (3, NCLASS), jnp.float32, -0.9, 0.9), -0.9, 0.9)
    return dict(iterate=iterate, forcing=forcing, start_field=start_field, classes=classes, open_mask=open_mask, diffusivity=diffusivity, drift=drift)


ALPHA = 0.1


def step_tables(length):
    index = jnp.arange(length, dtype=jnp.int32)
    folded = (index[:, None] * index[None, :]) % length
    angle = folded.astype(jnp.float32) * (2.0 * math.pi / length)
    cosine = jnp.cos(angle)
    sine = jnp.sin(angle)
    ramp = jnp.exp(index.astype(jnp.float32) * (math.log(ALPHA) / length))
    forward_re = cosine * ramp[None, :]
    forward_im = -sine * ramp[None, :]
    back_re = cosine / (ramp[:, None] * length)
    back_im = -sine / (ramp[:, None] * length)
    root = math.exp(math.log(ALPHA) / length)
    base = index.astype(jnp.float32) * (2.0 * math.pi / length)
    shift_re = 1.0 - root * jnp.cos(base)
    shift_im = root * jnp.sin(base)
    return forward_re, forward_im, back_re, back_im, shift_re, shift_im


def coefficients(classes, open_mask, diffusivity, drift):
    kappa = jnp.zeros(classes.shape, jnp.float32)
    tilt_x = jnp.zeros(classes.shape, jnp.float32)
    tilt_y = jnp.zeros(classes.shape, jnp.float32)
    tilt_z = jnp.zeros(classes.shape, jnp.float32)
    for level in range(diffusivity.shape[0]):
        match = classes == level
        kappa = jnp.where(match, diffusivity[level], kappa)
        tilt_x = jnp.where(match, drift[0, level], tilt_x)
        tilt_y = jnp.where(match, drift[1, level], tilt_y)
        tilt_z = jnp.where(match, drift[2, level], tilt_z)
    weight = open_mask.astype(jnp.float32)
    return weight, kappa, kappa * tilt_x, kappa * tilt_y, kappa * tilt_z


def couple(padded, kappa, flow_x, flow_y, flow_z):
    east = padded[..., 2:, 1:-1, 1:-1]
    west = padded[..., :-2, 1:-1, 1:-1]
    north = padded[..., 1:-1, 2:, 1:-1]
    south = padded[..., 1:-1, :-2, 1:-1]
    upper = padded[..., 1:-1, 1:-1, 2:]
    lower = padded[..., 1:-1, 1:-1, :-2]
    total = kappa * (east + west + north + south + upper + lower)
    return total - flow_x * (east - west) - flow_y * (north - south) - flow_z * (upper - lower)


def solve(source, shift_re, shift_im, weight, kappa, flow_x, flow_y, flow_z, extend):
    real_part = shift_re + 6.0 * kappa
    norm = real_part * real_part + shift_im * shift_im
    inv_re = real_part / norm
    inv_im = -shift_im / norm

    def update(total):
        return jnp.stack([weight * (total[0] * inv_re - total[1] * inv_im),
                          weight * (total[0] * inv_im + total[1] * inv_re)])

    field = update(source)
    for sweep in range(SWEEPS):
        field = update(source + couple(extend(field), kappa, flow_x, flow_y, flow_z))
    return field


def pad_grid(field):
    return jnp.pad(field, ((0, 0), (1, 1), (1, 1), (1, 1)))


def reference(iterate, forcing, start_field, classes, open_mask, diffusivity, drift):
    weight, kappa, flow_x, flow_y, flow_z = coefficients(classes, open_mask, diffusivity, drift)
    previous = jnp.concatenate([start_field[None], iterate[:-1]], axis=0)
    masked = iterate * weight
    applied = weight * (6.0 * kappa * masked - couple(pad_grid(masked), kappa, flow_x, flow_y, flow_z))
    residual = weight * (forcing + previous - iterate) - applied
    forward_re, forward_im, back_re, back_im, shift_re, shift_im = step_tables(L)
    flat = residual.reshape(L, -1)
    spec_re = jnp.dot(forward_re, flat, precision=lax.Precision.HIGHEST).reshape(residual.shape)
    spec_im = jnp.dot(forward_im, flat, precision=lax.Precision.HIGHEST).reshape(residual.shape)
    spectrum = jnp.stack([spec_re, spec_im], axis=1)

    def one(inputs):
        sre, sim, source = inputs
        return solve(source, sre, sim, weight, kappa, flow_x, flow_y, flow_z, pad_grid)

    solved = lax.map(one, (shift_re, shift_im, spectrum))
    part_re = solved[:, 0].reshape(L, -1)
    part_im = solved[:, 1].reshape(L, -1)
    corrected = jnp.dot(back_re, part_re, precision=lax.Precision.HIGHEST) + jnp.dot(back_im, part_im, precision=lax.Precision.HIGHEST)
    return residual, corrected.reshape(residual.shape)
```

```python
import functools
import math

import jax
import jax.numpy as jnp
import numpy as np
from jax import lax
from jax.experimental import pallas as pl
from jax.experimental.pallas import tpu as pltpu
from jax.sharding import PartitionSpec as P

SWEEPS = 4
ALPHA = 0.1
PAD = 8
MESH = pl.DeviceIdType.MESH


def step_tables(length, shares):
    half = length // 2
    planes = length // shares
    own = planes // 2
    index = np.arange(length)
    ramp = ALPHA ** (index / length)
    freq = np.arange(half)
    angle = 2.0 * math.pi * ((freq[:, None] * index[None, :]) % length) / length
    other = np.cos(math.pi * index)
    f_re, f_im = np.cos(angle), -np.sin(angle)
    f_im[0] = other
    scale = np.where(freq == 0, 1.0, 2.0)[:, None]
    b_re, b_im = scale * f_re, scale * f_im
    order = lambda re, im: np.stack([re.reshape(shares, own, -1), im.reshape(shares, own, -1)], 1).reshape(length, -1)
    forward = order(f_re, f_im) * ramp[None, :]
    back = (order(b_re, b_im) / (ramp[None, :] * length)).T
    root = ALPHA ** (1.0 / length)
    base = 2.0 * math.pi * freq / length
    re = 1.0 - root * np.cos(base)
    second = re.copy()
    second[0] = 1.0 + root
    im = root * np.sin(base)
    shifts = np.stack([re, second, im])[:, :, None].astype(np.float32)
    return forward.astype(np.float32), back.astype(np.float32), shifts


def kernel(T, S, it_ref, fc_ref, start_ref, cm_ref, diff_ref, drift_ref, fwd_ref, back_ref, shift_ref,
           res_ref, cor_ref,
           masked, last, arrived, cA, cB, xe, xw, xin, xout, xc, own_c, tin, spec, src, f0, f1,
           sol_c, inv, spec2, outb, ssem, rsem):
    NY, N, NZ = it_ref.shape
    L = N * T
    RB, Q = NY // T, T // S
    XB = Q * RB
    G = L // S
    H = G // 2
    W = SWEEPS
    R = RB + 2 * W
    t, s = lax.axis_index("tm"), lax.axis_index("space")

    barrier = pltpu.get_barrier_semaphore()
    for k in range(1, S):
        pl.semaphore_signal(barrier, inc=1, device_id={"space": lax.rem(s + k, S)}, device_id_type=MESH)
    for k in range(1, T):
        pl.semaphore_signal(barrier, inc=1, device_id={"tm": lax.rem(t + k, T)}, device_id_type=MESH)

    used = [0]
    sent = []

    def remote(a, b, where):
        at = used[0]
        used[0] += 1
        copy = pltpu.make_async_remote_copy(src_ref=a, dst_ref=b, send_sem=ssem.at[at], recv_sem=rsem.at[at],
                                            device_id=where, device_id_type=MESH)
        copy.start()
        sent.append(copy)
        return copy

    def table(cls, ref_row):
        out = jnp.zeros(cls.shape, jnp.float32)
        for level in range(diff_ref.shape[0]):
            out = jnp.where(cls == level, ref_row(level), out)
        return out

    def mult(v, m):
        return pl.multiple_of(v, m)

    lane = lax.broadcasted_iota(jnp.int32, (1, NZ), 1)
    not_top = jnp.where(lane < NZ - 1, 1.0, 0.0)
    not_low = jnp.where(lane > 0, 1.0, 0.0)

    cls = cm_ref[0, PAD:PAD + NY, :]
    own_c[0] = cm_ref[1, PAD:PAD + NY, :].astype(jnp.float32)
    kappa = table(cls, lambda i: diff_ref[i])
    fy = kappa * table(cls, lambda i: drift_ref[1, i])
    fz = kappa * table(cls, lambda i: drift_ref[2, i])
    own_c[1] = 6.0 * kappa
    own_c[2] = kappa - fy
    own_c[3] = kappa + fy
    own_c[4] = (kappa - fz) * not_top
    own_c[5] = (kappa + fz) * not_low
    zero = jnp.zeros((N, NZ), jnp.float32)
    masked[0] = zero
    masked[NY + 1] = zero

    def mask_row(r, c):
        masked[r + 1] = it_ref[r] * own_c[0, pl.ds(r, 1), :]
        return c

    lax.fori_loop(0, NY, mask_row, 0, unroll=8)
    last[...] = it_ref[:, N - 1, :]

    pl.semaphore_wait(barrier, S - 1 + T - 1)

    cpA = [remote(cm_ref.at[:, pl.ds(mult(lax.rem(s + k, S) * XB + PAD, 8), XB)], cA.at[s],
                  {"space": lax.rem(s + k, S)}) for k in range(1, S)]
    there = []
    for jj in range(Q):
        j = lax.rem(t + jj, Q)
        there.append([remote(masked.at[pl.ds((Q * lax.rem(s + k, S) + j) * RB + 1, RB)],
                             xin.at[s, pl.ds(jj * RB, RB)], {"space": lax.rem(s + k, S)}) for k in range(1, S)])
    cpL = remote(last, arrived, {"tm": lax.rem(t + 1, T)})
    cpB = [remote(cm_ref.at[:, pl.ds(mult(RB * t, 8), RB + 2 * PAD)], cB.at[s], {"space": lax.rem(s + k, S)})
           for k in range(1, S)]

    cA[s] = cm_ref[:, pl.ds(mult(s * XB + PAD, 8), XB), :]
    cB[s] = cm_ref[:, pl.ds(mult(RB * t, 8), RB + 2 * PAD), :]
    for jj in range(Q):
        j = lax.rem(t + jj, Q)
        xin[s, pl.ds(jj * RB, RB)] = masked[pl.ds((Q * s + j) * RB + 1, RB)]
    for cp in cpA:
        cp.wait_recv()

    def x_coefficients(x, c):
        cls = cA[x, 0]
        kappa = table(cls, lambda i: diff_ref[i])
        fx = kappa * table(cls, lambda i: drift_ref[0, i])
        xe[x] = kappa - fx
        xw[x] = kappa + fx
        return c

    lax.fori_loop(0, S, x_coefficients, 0)

    backs = []
    for jj in range(Q):
        j = lax.rem(t + jj, Q)
        for cp in there[jj]:
            cp.wait_recv()

        def x_row(r, c):
            at = jj * RB + r
            row = j * RB + r
            for x in range(S):
                total = None
                if x + 1 < S:
                    total = xe[x, pl.ds(row, 1), :] * xin[x + 1, at]
                if x > 0:
                    term = xw[x, pl.ds(row, 1), :] * xin[x - 1, at]
                    total = term if total is None else total + term
                xout[x, at] = zero if total is None else total
            return c

        lax.fori_loop(0, RB, x_row, 0, unroll=4)
        backs.append([remote(xout.at[lax.rem(s + k, S), pl.ds(jj * RB, RB)], xc.at[pl.ds((Q * s + j) * RB, RB)],
                             {"space": lax.rem(s + k, S)}) for k in range(1, S)])
        xc[pl.ds((Q * s + j) * RB, RB)] = xout[s, pl.ds(jj * RB, RB)]

    cpL.wait_recv()
    cpL.wait_send()
    sent[:] = [copy for copy in sent if copy is not cpL]
    last[...] = jnp.where(t == 0, start_ref[...], arrived[...])
    first = lax.broadcasted_iota(jnp.int32, (N, NZ), 0) == 0

    def residual_row(r):
        it = it_ref[r]
        mk = masked[r + 1]
        co = lambda i: own_c[i, pl.ds(r, 1), :]
        previous = jnp.where(first, last[pl.ds(r, 1), :], pltpu.roll(it, 1, 0))
        cpl = co(2) * masked[r + 2] + co(3) * masked[r] + xc[r]
        cpl = cpl + co(4) * pltpu.roll(mk, NZ - 1, 1) + co(5) * pltpu.roll(mk, 1, 1)
        return co(0) * ((fc_ref[r] + previous - it) - (co(1) * mk - cpl))

    tms = []
    for jj in range(Q):
        for cp in backs[jj]:
            cp.wait_recv()
        for m in list(range(1, S)) + [0]:
            k = jj + Q * m
            to = lax.rem(t + k, T)

            def one(r, c):
                res_ref[to * RB + r] = residual_row(to * RB + r)
                return c

            lax.fori_loop(0, RB, one, 0, unroll=4)
            if k:
                tms.append(remote(res_ref.at[pl.ds(to * RB, RB)], tin.at[:, pl.ds(mult(N * t, 8), N), :], {"tm": to}))
            else:
                tin[:, pl.ds(mult(N * t, 8), N), :] = res_ref[pl.ds(to * RB, RB)]

    for cp in cpB:
        cp.wait_recv()

    def solve_coefficients(x, c):
        cls = cB[x, 0]
        kappa = table(cls, lambda i: diff_ref[i])
        fx = kappa * table(cls, lambda i: drift_ref[0, i])
        fy = kappa * table(cls, lambda i: drift_ref[1, i])
        fz = kappa * table(cls, lambda i: drift_ref[2, i])
        sol_c[0, x] = kappa - fx
        sol_c[1, x] = kappa + fx
        sol_c[2, x] = kappa - fy
        sol_c[3, x] = kappa + fy
        sol_c[4, x] = (kappa - fz) * not_top
        sol_c[5, x] = (kappa + fz) * not_low
        sol_c[6, x] = cB[x, 1].astype(jnp.float32)
        sol_c[7, x] = 6.0 * kappa
        return c

    lax.fori_loop(0, S, solve_coefficients, 0)
    own = pl.ds(mult(s * H, 8) if H % 8 == 0 else s * H, H)
    sh_re, sh_second, sh_im = shift_ref[0, own], shift_ref[1, own], shift_ref[2, own]

    def inverse_row(r, c):
        for x in range(S):
            k6 = sol_c[7, x, pl.ds(r + PAD - W, 1), :]
            w = sol_c[6, x, pl.ds(r + PAD - W, 1), :]
            a, b = sh_re + k6, sh_second + k6
            na = w / (a * a + sh_im * sh_im)
            nb = w / (b * b + sh_im * sh_im)
            inv[0, x, r] = a * na
            inv[1, x, r] = -sh_im * na
            inv[2, x, r] = b * nb
        return c

    lax.fori_loop(0, R, inverse_row, 0)

    for cp in tms:
        cp.wait_recv()

    def transform(matrix_ref, a, b):
        group = 4 if RB % 4 == 0 else 1
        for g in range(0, RB, group):
            wide = jnp.concatenate([a[g + i] for i in range(group)], axis=1)
            wide = jnp.dot(matrix_ref[...], wide, precision=lax.Precision.HIGHEST, preferred_element_type=jnp.float32)
            for i in range(group):
                b[g + i] = wide[:, i * NZ:(i + 1) * NZ]

    transform(fwd_ref, tin, spec)
    def planes(who):
        return pl.ds(mult(G * who, 8), G)

    cps = [remote(spec.at[:, planes(lax.rem(s + k, S)), :], src.at[s, pl.ds(W, RB)], {"space": lax.rem(s + k, S)})
           for k in range(1, S)]
    src[s, pl.ds(W, RB)] = spec[:, planes(s), :]
    for cp in cps:
        cp.wait_recv()
    halos = [remote(src.at[:, pl.ds(W, W)], src.at[:, pl.ds(RB + W, W)], {"tm": lax.rem(t + T - 1, T)}),
             remote(src.at[:, pl.ds(RB, W)], src.at[:, pl.ds(0, W)], {"tm": lax.rem(t + 1, T)})]

    def update(x, r, total, out):
        re, im = total[:H], total[H:]
        a, b, d = inv[0, x, r], inv[1, x, r], inv[2, x, r]
        out[x, r] = jnp.concatenate([re * a - im * b, re * b + im * d], axis=0)

    def first_row(r, c):
        for x in range(S):
            update(x, r, src[x, r], f0)
        return c

    lax.fori_loop(W, W + RB, first_row, 0, unroll=2)
    for cp in halos:
        cp.wait_recv()
    lax.fori_loop(0, W, first_row, 0, unroll=2)
    lax.fori_loop(W + RB, R, first_row, 0, unroll=2)

    old, new = f0, f1
    for sweep in range(1, SWEEPS + 1):
        def sweep_row(r, c):
            for x in range(S):
                co = lambda i: sol_c[i, x, pl.ds(r + PAD - W, 1), :]
                mid = old[x, r]
                total = src[x, r] + co(2) * old[x, r + 1] + co(3) * old[x, r - 1]
                total = total + co(4) * pltpu.roll(mid, NZ - 1, 1) + co(5) * pltpu.roll(mid, 1, 1)
                if x + 1 < S:
                    total = total + co(0) * old[x + 1, r]
                if x > 0:
                    total = total + co(1) * old[x - 1, r]
                update(x, r, total, new)
            return c

        lax.fori_loop(sweep, R - sweep, sweep_row, 0, unroll=2)
        old, new = new, old

    cps = [remote(old.at[lax.rem(s + k, S), pl.ds(W, RB)], spec2.at[:, planes(s), :], {"space": lax.rem(s + k, S)})
           for k in range(1, S)]
    spec2[:, planes(s), :] = old[s, pl.ds(W, RB)]
    for cp in cps:
        cp.wait_recv()
    transform(back_ref, spec2, outb)
    cps = []
    for k in range(1, T):
        to = lax.rem(t + k, T)
        cps.append(remote(outb.at[:, pl.ds(mult(N * to, 8), N), :], cor_ref.at[pl.ds(RB * t, RB)], {"tm": to}))
    cor_ref[pl.ds(RB * t, RB)] = outb[:, pl.ds(mult(N * t, 8), N), :]
    for cp in cps:
        cp.wait_recv()
    for cp in sent:
        cp.wait_send()


def local(T, S, iterate, forcing, start_field, classes, open_mask, diffusivity, drift):
    N, _, NY, NZ = iterate.shape
    L = N * T
    RB, Q = NY // T, T // S
    XB, G = Q * RB, L // S
    H, W = G // 2, SWEEPS
    R = RB + 2 * W
    fwd, back, shifts = step_tables(L, S)
    shifts = np.ascontiguousarray(np.broadcast_to(shifts, (3, L // 2, NZ)))
    it = jnp.swapaxes(iterate[:, 0], 0, 1)
    fc = jnp.swapaxes(forcing[:, 0], 0, 1)
    cm = jnp.pad(jnp.concatenate([classes, open_mask], 0), ((0, 0), (PAD, PAD), (0, 0)))
    copies = 3 * (S - 1) + 1 + 2 * Q * (S - 1) + (S - 1) + 2 + 2 * (T - 1)
    f32 = jnp.float32
    vmem = lambda *shape: pltpu.VMEM(shape, f32)
    VM, SM = pl.BlockSpec(memory_space=pltpu.VMEM), pl.BlockSpec(memory_space=pltpu.SMEM)
    res, cor = pl.pallas_call(
        functools.partial(kernel, T, S),
        out_shape=[jax.ShapeDtypeStruct((NY, N, NZ), f32)] * 2,
        in_specs=[VM, VM, VM, VM, SM, SM, VM, VM, VM],
        out_specs=[VM, VM],
        scratch_shapes=[
            vmem(NY + 2, N, NZ), vmem(NY, NZ), vmem(NY, NZ),
            pltpu.VMEM((S, 2, XB, NZ), jnp.int32), pltpu.VMEM((S, 2, RB + 2 * PAD, NZ), jnp.int32),
            vmem(S, XB, NZ), vmem(S, XB, NZ), vmem(S, XB, N, NZ), vmem(S, XB, N, NZ), vmem(NY, N, NZ),
            vmem(6, NY, NZ), vmem(RB, L, NZ), vmem(RB, L, NZ),
            vmem(S, R, G, NZ), vmem(S, R, G, NZ), vmem(S, R, G, NZ),
            vmem(8, S, RB + 2 * PAD, NZ), vmem(3, S, R, H, NZ), vmem(RB, L, NZ), vmem(RB, L, NZ),
            pltpu.SemaphoreType.DMA((copies,)), pltpu.SemaphoreType.DMA((copies,)),
        ],
        compiler_params=pltpu.CompilerParams(collective_id=0, has_side_effects=True, vmem_limit_bytes=48 * 2**20),
        name="all_at_once",
    )(it, fc, start_field[0], cm, diffusivity, drift, fwd, back, shifts)
    return jnp.swapaxes(res, 0, 1)[:, None], jnp.swapaxes(cor, 0, 1)[:, None]


def solution(mesh):
    field, cells = P("tm", "space", None, None), P("space", None, None)
    return jax.shard_map(
        functools.partial(local, mesh.shape["tm"], mesh.shape["space"]),
        mesh=mesh,
        in_specs=(field, field, cells, cells, cells, P(), P()),
        out_specs=(field, field),
        check_vma=False,
    )
```

```python
import functools
import math

import jax
import jax.numpy as jnp
import numpy as np
from jax import lax
from jax.experimental import pallas as pl
from jax.experimental.pallas import tpu as pltpu
from jax.sharding import PartitionSpec as P

SWEEPS = 4
ALPHA = 0.1
PAD = 8
MESH = pl.DeviceIdType.MESH


def step_tables(length, shares):
    half = length // 2
    planes = length // shares
    own = planes // 2
    index = np.arange(length)
    ramp = ALPHA ** (index / length)
    freq = np.arange(half)
    angle = 2.0 * math.pi * ((freq[:, None] * index[None, :]) % length) / length
    other = np.cos(math.pi * index)
    f_re, f_im = np.cos(angle), -np.sin(angle)
    f_im[0] = other
    scale = np.where(freq == 0, 1.0, 2.0)[:, None]
    b_re, b_im = scale * f_re, scale * f_im
    order = lambda re, im: np.stack([re.reshape(shares, own, -1), im.reshape(shares, own, -1)], 1).reshape(length, -1)
    forward = order(f_re, f_im) * ramp[None, :]
    back = (order(b_re, b_im) / (ramp[None, :] * length)).T
    root = ALPHA ** (1.0 / length)
    base = 2.0 * math.pi * freq / length
    re = 1.0 - root * np.cos(base)
    second = re.copy()
    second[0] = 1.0 + root
    im = root * np.sin(base)
    shifts = np.stack([re, second, im])[:, :, None].astype(np.float32)
    return forward.astype(np.float32), back.astype(np.float32), shifts


def kernel(T, S, it_ref, fc_ref, start_ref, cls_ref, open_ref, diff_ref, drift_ref, fwd_ref, back_ref, shift_ref,
           res_ref, cor_ref,
           cm_ref, masked, last, arrived, cA, cB, xe, xw, xin, xout, xc, own_c, tin, spec, src, f0, f1,
           sol_c, inv, spec2, outb, ssem, rsem):
    NY, N, NZ = it_ref.shape
    L = N * T
    RB, Q = NY // T, T // S
    XB = Q * RB
    G = L // S
    H = G // 2
    W = SWEEPS
    R = RB + 2 * W
    C = RB // W
    chunks = [0, C - 1] + list(range(1, C - 1))
    t, s = lax.axis_index("tm"), lax.axis_index("space")

    barrier = pltpu.get_barrier_semaphore()
    for k in range(1, S):
        pl.semaphore_signal(barrier, inc=1, device_id={"space": lax.rem(s + k, S)}, device_id_type=MESH)
    for k in range(1, T):
        pl.semaphore_signal(barrier, inc=1, device_id={"tm": lax.rem(t + k, T)}, device_id_type=MESH)

    used = [0]
    sent = []

    def remote(a, b, where):
        at = used[0]
        used[0] += 1
        copy = pltpu.make_async_remote_copy(src_ref=a, dst_ref=b, send_sem=ssem.at[at], recv_sem=rsem.at[at],
                                            device_id=where, device_id_type=MESH)
        copy.start()
        sent.append(copy)
        return copy

    def table(cls, ref_row):
        out = jnp.zeros(cls.shape, jnp.float32)
        for level in range(diff_ref.shape[0]):
            out = jnp.where(cls == level, ref_row(level), out)
        return out

    def mult(v, m):
        return pl.multiple_of(v, m)

    lane = lax.broadcasted_iota(jnp.int32, (1, NZ), 1)
    not_top = jnp.where(lane < NZ - 1, 1.0, 0.0)
    not_low = jnp.where(lane > 0, 1.0, 0.0)

    edge = jnp.zeros((PAD, NZ), jnp.int32)
    for i, ref in enumerate((cls_ref, open_ref)):
        cm_ref[i, 0:PAD, :] = edge
        cm_ref[i, PAD + NY:, :] = edge
        cm_ref[i, PAD:PAD + NY, :] = ref[...]
    cls = cls_ref[...]
    own_c[0] = open_ref[...].astype(jnp.float32)
    kappa = table(cls, lambda i: diff_ref[i])
    fy = kappa * table(cls, lambda i: drift_ref[1, i])
    fz = kappa * table(cls, lambda i: drift_ref[2, i])
    own_c[1] = 6.0 * kappa
    own_c[2] = kappa - fy
    own_c[3] = kappa + fy
    own_c[4] = (kappa - fz) * not_top
    own_c[5] = (kappa + fz) * not_low
    zero = jnp.zeros((N, NZ), jnp.float32)
    masked[0] = zero
    masked[NY + 1] = zero

    def mask_row(r, c):
        masked[r + 1] = it_ref[r] * own_c[0, pl.ds(r, 1), :]
        return c

    lax.fori_loop(0, NY, mask_row, 0, unroll=8)
    last[...] = it_ref[:, N - 1, :]

    pl.semaphore_wait(barrier, S - 1 + T - 1)

    cpA = [remote(cm_ref.at[:, pl.ds(mult(lax.rem(s + k, S) * XB + PAD, 8), XB)], cA.at[s],
                  {"space": lax.rem(s + k, S)}) for k in range(1, S)]
    pieces = [(c, jj) for c in chunks for jj in range(Q)]
    there = []
    for c, jj in pieces:
        j = lax.rem(t + jj, Q)
        there.append([remote(masked.at[pl.ds((Q * lax.rem(s + k, S) + j) * RB + c * W + 1, W)],
                             xin.at[s, pl.ds(jj * RB + c * W, W)], {"space": lax.rem(s + k, S)}) for k in range(1, S)])
    cpL = remote(last, arrived, {"tm": lax.rem(t + 1, T)})
    cpB = [remote(cm_ref.at[:, pl.ds(mult(RB * t, 8), RB + 2 * PAD)], cB.at[s], {"space": lax.rem(s + k, S)})
           for k in range(1, S)]

    cA[s] = cm_ref[:, pl.ds(mult(s * XB + PAD, 8), XB), :]
    cB[s] = cm_ref[:, pl.ds(mult(RB * t, 8), RB + 2 * PAD), :]
    for jj in range(Q):
        j = lax.rem(t + jj, Q)
        xin[s, pl.ds(jj * RB, RB)] = masked[pl.ds((Q * s + j) * RB + 1, RB)]
    for cp in cpA:
        cp.wait_recv()

    def x_coefficients(x, c):
        cls = cA[x, 0]
        kappa = table(cls, lambda i: diff_ref[i])
        fx = kappa * table(cls, lambda i: drift_ref[0, i])
        xe[x] = kappa - fx
        xw[x] = kappa + fx
        return c

    lax.fori_loop(0, S, x_coefficients, 0)

    backs = []
    for (c, jj), copies in zip(pieces, there):
        j = lax.rem(t + jj, Q)
        for cp in copies:
            cp.wait_recv()
        base = jj * RB + c * W
        for r in range(W):
            row = j * RB + c * W + r
            fields = [xin[x, base + r] for x in range(S)]
            for x in range(S):
                total = None
                if x + 1 < S:
                    total = xe[x, pl.ds(row, 1), :] * fields[x + 1]
                if x > 0:
                    term = xw[x, pl.ds(row, 1), :] * fields[x - 1]
                    total = term if total is None else total + term
                xout[x, base + r] = zero if total is None else total
        home = pl.ds((Q * s + j) * RB + c * W, W)
        backs.append([remote(xout.at[lax.rem(s + k, S), pl.ds(base, W)], xc.at[home], {"space": lax.rem(s + k, S)})
                      for k in range(1, S)])
        xc[home] = xout[s, pl.ds(base, W)]

    cpL.wait_recv()
    cpL.wait_send()
    sent[:] = [copy for copy in sent if copy is not cpL]
    last[...] = jnp.where(t == 0, start_ref[...], arrived[...])
    first = lax.broadcasted_iota(jnp.int32, (N, NZ), 0) == 0

    def residual_row(r):
        it = it_ref[r]
        mk = masked[r + 1]
        co = lambda i: own_c[i, pl.ds(r, 1), :]
        previous = jnp.where(first, last[pl.ds(r, 1), :], pltpu.roll(it, 1, 0))
        cpl = co(2) * masked[r + 2] + co(3) * masked[r] + xc[r]
        cpl = cpl + co(4) * pltpu.roll(mk, NZ - 1, 1) + co(5) * pltpu.roll(mk, 1, 1)
        return co(0) * ((fc_ref[r] + previous - it) - (co(1) * mk - cpl))

    tms = {c: [] for c in chunks}
    for (c, jj), copies in zip(pieces, backs):
        for cp in copies:
            cp.wait_recv()
        for m in list(range(1, S)) + [0]:
            k = jj + Q * m
            to = lax.rem(t + k, T)
            at = to * RB + c * W
            for r in range(W):
                res_ref[at + r] = residual_row(at + r)
            here = tin.at[pl.ds(c * W, W), pl.ds(mult(N * t, 8), N), :]
            if k:
                tms[c].append(remote(res_ref.at[pl.ds(at, W)], here, {"tm": to}))
            else:
                here[...] = res_ref[pl.ds(at, W)]

    for cp in cpB:
        cp.wait_recv()

    def solve_coefficients(x, c):
        cls = cB[x, 0]
        kappa = table(cls, lambda i: diff_ref[i])
        fx = kappa * table(cls, lambda i: drift_ref[0, i])
        fy = kappa * table(cls, lambda i: drift_ref[1, i])
        fz = kappa * table(cls, lambda i: drift_ref[2, i])
        sol_c[0, x] = kappa - fx
        sol_c[1, x] = kappa + fx
        sol_c[2, x] = kappa - fy
        sol_c[3, x] = kappa + fy
        sol_c[4, x] = (kappa - fz) * not_top
        sol_c[5, x] = (kappa + fz) * not_low
        sol_c[6, x] = cB[x, 1].astype(jnp.float32)
        sol_c[7, x] = 6.0 * kappa
        return c

    lax.fori_loop(0, S, solve_coefficients, 0)
    own = pl.ds(mult(s * H, 8) if H % 8 == 0 else s * H, H)
    sh_re, sh_second, sh_im = shift_ref[0, own], shift_ref[1, own], shift_ref[2, own]

    def inverse_row(r, c):
        for x in range(S):
            k6 = sol_c[7, x, pl.ds(r + PAD - W, 1), :]
            w = sol_c[6, x, pl.ds(r + PAD - W, 1), :]
            a, b = sh_re + k6, sh_second + k6
            na = w / (a * a + sh_im * sh_im)
            nb = w / (b * b + sh_im * sh_im)
            inv[0, x, r] = a * na
            inv[1, x, r] = -sh_im * na
            inv[2, x, r] = b * nb
        return c

    lax.fori_loop(0, R, inverse_row, 0)

    def transform(matrix_ref, a, b, c):
        wide = jnp.concatenate([a[c * W + i] for i in range(W)], axis=1)
        wide = jnp.dot(matrix_ref[...], wide, precision=lax.Precision.HIGHEST, preferred_element_type=jnp.float32)
        for i in range(W):
            b[c * W + i] = wide[:, i * NZ:(i + 1) * NZ]

    def planes(who):
        return pl.ds(mult(G * who, 8), G)

    def update(x, r, total, out):
        re, im = total[:H], total[H:]
        a, b, d = inv[0, x, r], inv[1, x, r], inv[2, x, r]
        out[x, r] = jnp.concatenate([re * a - im * b, re * b + im * d], axis=0)

    def first_row(r, c):
        for x in range(S):
            update(x, r, src[x, r], f0)
        return c

    halos = []

    def land(c, copies):
        for cp in copies:
            cp.wait_recv()
        if c == 0:
            halos.append(remote(src.at[:, pl.ds(W, W)], src.at[:, pl.ds(RB + W, W)], {"tm": lax.rem(t + T - 1, T)}))
        if c == C - 1:
            halos.append(remote(src.at[:, pl.ds(RB, W)], src.at[:, pl.ds(0, W)], {"tm": lax.rem(t + 1, T)}))
        lax.fori_loop(W + c * W, W + c * W + W, first_row, 0, unroll=2)

    flying = []
    for c in chunks:
        for cp in tms[c]:
            cp.wait_recv()
        transform(fwd_ref, tin, spec, c)
        rows, there_rows = pl.ds(c * W, W), pl.ds(W + c * W, W)
        copies = [remote(spec.at[rows, planes(lax.rem(s + k, S)), :], src.at[s, there_rows],
                         {"space": lax.rem(s + k, S)}) for k in range(1, S)]
        src[s, there_rows] = spec[rows, planes(s), :]
        if flying:
            land(*flying.pop())
        flying.append((c, copies))
    land(*flying.pop())
    for cp in halos:
        cp.wait_recv()
    lax.fori_loop(0, W, first_row, 0, unroll=2)
    lax.fori_loop(W + RB, R, first_row, 0, unroll=2)

    old, new = f0, f1
    solved = []
    for sweep in range(1, SWEEPS + 1):
        def sweep_row(r, c):
            mids = [old[x, r] for x in range(S)]
            for x in range(S):
                co = lambda i: sol_c[i, x, pl.ds(r + PAD - W, 1), :]
                total = src[x, r] + co(2) * old[x, r + 1] + co(3) * old[x, r - 1]
                total = total + co(4) * pltpu.roll(mids[x], NZ - 1, 1) + co(5) * pltpu.roll(mids[x], 1, 1)
                if x + 1 < S:
                    total = total + co(0) * mids[x + 1]
                if x > 0:
                    total = total + co(1) * mids[x - 1]
                update(x, r, total, new)
            return c

        if sweep < SWEEPS:
            lax.fori_loop(sweep, R - sweep, sweep_row, 0, unroll=2)
        else:
            for c in range(C):
                lax.fori_loop(W + c * W, W + c * W + W, sweep_row, 0, unroll=2)
                rows, from_rows = pl.ds(c * W, W), pl.ds(W + c * W, W)
                solved.append([remote(new.at[lax.rem(s + k, S), from_rows], spec2.at[rows, planes(s), :],
                                      {"space": lax.rem(s + k, S)}) for k in range(1, S)])
                spec2[rows, planes(s), :] = new[s, from_rows]
        old, new = new, old

    final = []
    for c in range(C):
        for cp in solved[c]:
            cp.wait_recv()
        transform(back_ref, spec2, outb, c)
        rows, home = pl.ds(c * W, W), pl.ds(RB * t + c * W, W)
        for k in range(1, T):
            to = lax.rem(t + k, T)
            final.append(remote(outb.at[rows, pl.ds(mult(N * to, 8), N), :], cor_ref.at[home], {"tm": to}))
        cor_ref[home] = outb[rows, pl.ds(mult(N * t, 8), N), :]
    for cp in final:
        cp.wait_recv()
    for cp in sent:
        cp.wait_send()


def local(T, S, iterate, forcing, start_field, classes, open_mask, diffusivity, drift):
    N, _, NY, NZ = iterate.shape
    L = N * T
    RB, Q = NY // T, T // S
    XB, G = Q * RB, L // S
    H, W = G // 2, SWEEPS
    R = RB + 2 * W
    fwd, back, shifts = step_tables(L, S)
    shifts = np.ascontiguousarray(np.broadcast_to(shifts, (3, L // 2, NZ)))
    it = jnp.swapaxes(iterate[:, 0], 0, 1)
    fc = jnp.swapaxes(forcing[:, 0], 0, 1)
    C = RB // W
    copies = 2 * (S - 1) + 1 + 2 * C * Q * (S - 1) + 2 * C * (S - 1) + 2 + 2 * C * (T - 1)
    f32 = jnp.float32
    vmem = lambda *shape: pltpu.VMEM(shape, f32)
    VM, SM = pl.BlockSpec(memory_space=pltpu.VMEM), pl.BlockSpec(memory_space=pltpu.SMEM)
    res, cor = pl.pallas_call(
        functools.partial(kernel, T, S),
        out_shape=[jax.ShapeDtypeStruct((NY, N, NZ), f32)] * 2,
        in_specs=[VM, VM, VM, VM, VM, SM, SM, VM, VM, VM],
        out_specs=[VM, VM],
        scratch_shapes=[
            pltpu.VMEM((2, NY + 2 * PAD, NZ), jnp.int32), vmem(NY + 2, N, NZ), vmem(NY, NZ), vmem(NY, NZ),
            pltpu.VMEM((S, 2, XB, NZ), jnp.int32), pltpu.VMEM((S, 2, RB + 2 * PAD, NZ), jnp.int32),
            vmem(S, XB, NZ), vmem(S, XB, NZ), vmem(S, XB, N, NZ), vmem(S, XB, N, NZ), vmem(NY, N, NZ),
            vmem(6, NY, NZ), vmem(RB, L, NZ), vmem(RB, L, NZ),
            vmem(S, R, G, NZ), vmem(S, R, G, NZ), vmem(S, R, G, NZ),
            vmem(8, S, RB + 2 * PAD, NZ), vmem(3, S, R, H, NZ), vmem(RB, L, NZ), vmem(RB, L, NZ),
            pltpu.SemaphoreType.DMA((copies,)), pltpu.SemaphoreType.DMA((copies,)),
        ],
        compiler_params=pltpu.CompilerParams(collective_id=0, has_side_effects=True, vmem_limit_bytes=48 * 2**20),
        name="all_at_once",
    )(it, fc, start_field[0], classes[0], open_mask[0], diffusivity, drift, fwd, back, shifts)
    return jnp.swapaxes(res, 0, 1)[:, None], jnp.swapaxes(cor, 0, 1)[:, None]


def solution(mesh):
    field, cells = P("tm", "space", None, None), P("space", None, None)
    return jax.shard_map(
        functools.partial(local, mesh.shape["tm"], mesh.shape["space"]),
        mesh=mesh,
        in_specs=(field, field, cells, cells, cells, P(), P()),
        out_specs=(field, field),
        check_vma=False,
    )
```

```python
import functools
import math

import jax
import jax.numpy as jnp
import ml_dtypes
import numpy as np
from jax import lax
from jax.experimental import pallas as pl
from jax.experimental.pallas import tpu as pltpu
from jax.sharding import PartitionSpec as P

SWEEPS = 4
ALPHA = 0.1
PAD = 8
MESH = pl.DeviceIdType.MESH


def step_tables(length, shares):
    half = length // 2
    planes = length // shares
    own = planes // 2
    index = np.arange(length)
    ramp = ALPHA ** (index / length)
    freq = np.arange(half)
    angle = 2.0 * math.pi * ((freq[:, None] * index[None, :]) % length) / length
    other = np.cos(math.pi * index)
    f_re, f_im = np.cos(angle), -np.sin(angle)
    f_im[0] = other
    scale = np.where(freq == 0, 1.0, 2.0)[:, None]
    b_re, b_im = scale * f_re, scale * f_im
    order = lambda re, im: np.stack([re.reshape(shares, own, -1), im.reshape(shares, own, -1)], 1).reshape(length, -1)
    forward = order(f_re, f_im) * ramp[None, :]
    back = (order(b_re, b_im) / (ramp[None, :] * length)).T
    root = ALPHA ** (1.0 / length)
    base = 2.0 * math.pi * freq / length
    re = 1.0 - root * np.cos(base)
    second = re.copy()
    second[0] = 1.0 + root
    im = root * np.sin(base)
    shifts = np.stack([re, second, im])[:, :, None].astype(np.float32)
    return split_matrix(forward), split_matrix(back), shifts


def split_matrix(matrix):
    high = matrix.astype(ml_dtypes.bfloat16)
    low = (matrix - high.astype(np.float64)).astype(ml_dtypes.bfloat16)
    return np.concatenate([high, high, low], axis=1)


def kernel(T, S, it_in, fc_in, start_ref, cls_ref, open_ref, diff_ref, drift_ref, fwd_ref, back_ref, shift_ref,
           res_ref, cor_ref,
           it_ref, fc_ref, in_sem, cm_ref, masked, last, arrived, cA, cB, xe, xw, xin, xout, xc, own_c, tin, spec, src, f0, f1,
           sol_c, inv, spec2, outb, ssem, rsem):
    NY, N, NZ = it_ref.shape
    L = N * T
    RB, Q = NY // T, T // S
    XB = Q * RB
    G = L // S
    H = G // 2
    W = SWEEPS
    R = RB + 2 * W
    C = RB // W
    chunks = [0, C - 1] + list(range(1, C - 1))
    t, s = lax.axis_index("tm"), lax.axis_index("space")

    loads = []
    for i, (a, b) in enumerate(((it_in, it_ref), (fc_in, fc_ref))):
        loads.append([pltpu.make_async_copy(a.at[n], b.at[:, n, :], in_sem.at[i * N + n]) for n in range(N)])
        for copy in loads[i]:
            copy.start()

    barrier = pltpu.get_barrier_semaphore()
    for k in range(1, S):
        pl.semaphore_signal(barrier, inc=1, device_id={"space": lax.rem(s + k, S)}, device_id_type=MESH)
    for k in range(1, T):
        pl.semaphore_signal(barrier, inc=1, device_id={"tm": lax.rem(t + k, T)}, device_id_type=MESH)

    used = [0]
    sent = []

    def remote(a, b, where):
        at = used[0]
        used[0] += 1
        copy = pltpu.make_async_remote_copy(src_ref=a, dst_ref=b, send_sem=ssem.at[at], recv_sem=rsem.at[at],
                                            device_id=where, device_id_type=MESH)
        copy.start()
        sent.append(copy)
        return copy

    def table(cls, ref_row):
        out = jnp.zeros(cls.shape, jnp.float32)
        for level in range(diff_ref.shape[0]):
            out = jnp.where(cls == level, ref_row(level), out)
        return out

    def mult(v, m):
        return pl.multiple_of(v, m)

    lane = lax.broadcasted_iota(jnp.int32, (1, NZ), 1)
    not_top = jnp.where(lane < NZ - 1, 1.0, 0.0)
    not_low = jnp.where(lane > 0, 1.0, 0.0)

    edge = jnp.zeros((PAD, NZ), jnp.int32)
    for i, ref in enumerate((cls_ref, open_ref)):
        cm_ref[i, 0:PAD, :] = edge
        cm_ref[i, PAD + NY:, :] = edge
        cm_ref[i, PAD:PAD + NY, :] = ref[...]
    cls = cls_ref[...]
    own_c[0] = open_ref[...].astype(jnp.float32)
    kappa = table(cls, lambda i: diff_ref[i])
    fy = kappa * table(cls, lambda i: drift_ref[1, i])
    fz = kappa * table(cls, lambda i: drift_ref[2, i])
    own_c[1] = 6.0 * kappa
    own_c[2] = kappa - fy
    own_c[3] = kappa + fy
    own_c[4] = (kappa - fz) * not_top
    own_c[5] = (kappa + fz) * not_low
    zero = jnp.zeros((N, NZ), jnp.float32)
    masked[0] = zero
    masked[NY + 1] = zero

    for copy in loads[0]:
        copy.wait()

    def mask_row(r, c):
        masked[r + 1] = it_ref[r] * own_c[0, pl.ds(r, 1), :]
        return c

    lax.fori_loop(0, NY, mask_row, 0, unroll=8)

    pl.semaphore_wait(barrier, S - 1 + T - 1)

    cpA = [remote(cm_ref.at[:, pl.ds(mult(lax.rem(s + k, S) * XB + PAD, 8), XB)], cA.at[s],
                  {"space": lax.rem(s + k, S)}) for k in range(1, S)]
    pieces = [(c, jj) for c in chunks for jj in range(Q)]
    there = []

    def send_piece(c, jj):
        j = lax.rem(t + jj, Q)
        there.append([remote(masked.at[pl.ds((Q * lax.rem(s + k, S) + j) * RB + c * W + 1, W)],
                             xin.at[s, pl.ds(jj * RB + c * W, W)], {"space": lax.rem(s + k, S)}) for k in range(1, S)])
        xin[s, pl.ds(jj * RB + c * W, W)] = masked[pl.ds((Q * s + j) * RB + c * W + 1, W)]

    ahead, lag = 4, 2
    for piece in pieces[:ahead]:
        send_piece(*piece)
    cpL = remote(it_in.at[N - 1], arrived, {"tm": lax.rem(t + 1, T)})
    cpB = [remote(cm_ref.at[:, pl.ds(mult(RB * t, 8), RB + 2 * PAD)], cB.at[s], {"space": lax.rem(s + k, S)})
           for k in range(1, S)]

    cA[s] = cm_ref[:, pl.ds(mult(s * XB + PAD, 8), XB), :]
    cB[s] = cm_ref[:, pl.ds(mult(RB * t, 8), RB + 2 * PAD), :]
    for cp in cpA:
        cp.wait_recv()

    def x_coefficients(x, c):
        cls = cA[x, 0]
        kappa = table(cls, lambda i: diff_ref[i])
        fx = kappa * table(cls, lambda i: drift_ref[0, i])
        xe[x] = kappa - fx
        xw[x] = kappa + fx
        return c

    lax.fori_loop(0, S, x_coefficients, 0)

    backs = []

    def couple_piece(c, jj, copies):
        j = lax.rem(t + jj, Q)
        for cp in copies:
            cp.wait_recv()
        base = jj * RB + c * W
        for r in range(W):
            row = j * RB + c * W + r
            fields = [xin[x, base + r] for x in range(S)]
            for x in range(S):
                total = None
                if x + 1 < S:
                    total = xe[x, pl.ds(row, 1), :] * fields[x + 1]
                if x > 0:
                    term = xw[x, pl.ds(row, 1), :] * fields[x - 1]
                    total = term if total is None else total + term
                xout[x, base + r] = zero if total is None else total
        home = pl.ds((Q * s + j) * RB + c * W, W)
        backs.append([remote(xout.at[lax.rem(s + k, S), pl.ds(base, W)], xc.at[home], {"space": lax.rem(s + k, S)})
                      for k in range(1, S)])
        xc[home] = xout[s, pl.ds(base, W)]

    first = lax.broadcasted_iota(jnp.int32, (N, NZ), 0) == 0

    def residual_row(r):
        it = it_ref[r]
        mk = masked[r + 1]
        co = lambda i: own_c[i, pl.ds(r, 1), :]
        previous = jnp.where(first, last[pl.ds(r, 1), :], pltpu.roll(it, 1, 0))
        cpl = co(2) * masked[r + 2] + co(3) * masked[r] + xc[r]
        cpl = cpl + co(4) * pltpu.roll(mk, NZ - 1, 1) + co(5) * pltpu.roll(mk, 1, 1)
        return co(0) * ((fc_ref[r] + previous - it) - (co(1) * mk - cpl))

    tms = {c: [] for c in chunks}

    def residual_piece(c, jj, copies):
        for cp in copies:
            cp.wait_recv()
        for m in list(range(1, S)) + [0]:
            k = jj + Q * m
            to = lax.rem(t + k, T)
            at = to * RB + c * W
            for r in range(W):
                res_ref[at + r] = residual_row(at + r)
            here = tin.at[pl.ds(c * W, W), pl.ds(mult(N * t, 8), N), :]
            if k:
                tms[c].append(remote(res_ref.at[pl.ds(at, W)], here, {"tm": to}))
            else:
                here[...] = res_ref[pl.ds(at, W)]

    for i in range(len(pieces) + lag):
        if i < len(pieces):
            couple_piece(*pieces[i], there[i])
        if i + ahead < len(pieces):
            send_piece(*pieces[i + ahead])
        if i == lag - 1:
            cpL.wait_recv()
            last[...] = jnp.where(t == 0, start_ref[...], arrived[...])
            for copy in loads[1]:
                copy.wait()
        if i >= lag:
            residual_piece(*pieces[i - lag], backs[i - lag])

    for cp in cpB:
        cp.wait_recv()

    def solve_coefficients(x, c):
        cls = cB[x, 0]
        kappa = table(cls, lambda i: diff_ref[i])
        fx = kappa * table(cls, lambda i: drift_ref[0, i])
        fy = kappa * table(cls, lambda i: drift_ref[1, i])
        fz = kappa * table(cls, lambda i: drift_ref[2, i])
        sol_c[0, x] = kappa - fx
        sol_c[1, x] = kappa + fx
        sol_c[2, x] = kappa - fy
        sol_c[3, x] = kappa + fy
        sol_c[4, x] = (kappa - fz) * not_top
        sol_c[5, x] = (kappa + fz) * not_low
        sol_c[6, x] = cB[x, 1].astype(jnp.float32)
        sol_c[7, x] = 6.0 * kappa
        return c

    lax.fori_loop(0, S, solve_coefficients, 0)
    own = pl.ds(mult(s * H, 8) if H % 8 == 0 else s * H, H)
    sh_re, sh_second, sh_im = shift_ref[0, own], shift_ref[1, own], shift_ref[2, own]

    def inverse_row(r, c):
        for x in range(S):
            k6 = sol_c[7, x, pl.ds(r + PAD - W, 1), :]
            w = sol_c[6, x, pl.ds(r + PAD - W, 1), :]
            a, b = sh_re + k6, sh_second + k6
            na = w / (a * a + sh_im * sh_im)
            nb = w / (b * b + sh_im * sh_im)
            inv[0, x, r] = a * na
            inv[1, x, r] = -sh_im * na
            inv[2, x, r] = b * nb
        return c

    lax.fori_loop(0, R, inverse_row, 0)

    def transform(matrix_ref, a, b, c):
        wide = jnp.concatenate([a[c * W + i] for i in range(W)], axis=1)
        high = wide.astype(jnp.bfloat16)
        low = (wide - high.astype(jnp.float32)).astype(jnp.bfloat16)
        wide = jnp.dot(matrix_ref[...], jnp.concatenate([high, low, high], axis=0), preferred_element_type=jnp.float32)
        for i in range(W):
            b[c * W + i] = wide[:, i * NZ:(i + 1) * NZ]

    def planes(who):
        return pl.ds(mult(G * who, 8), G)

    def update(x, r, total, out):
        re, im = total[:H], total[H:]
        a, b, d = inv[0, x, r], inv[1, x, r], inv[2, x, r]
        out[x, r] = jnp.concatenate([re * a - im * b, re * b + im * d], axis=0)

    def first_row(r, c):
        for x in range(S):
            update(x, r, src[x, r], f0)
        return c

    halos = []

    def land(c, copies):
        for cp in copies:
            cp.wait_recv()
        if c == 0:
            halos.append(remote(src.at[:, pl.ds(W, W)], src.at[:, pl.ds(RB + W, W)], {"tm": lax.rem(t + T - 1, T)}))
        if c == C - 1:
            halos.append(remote(src.at[:, pl.ds(RB, W)], src.at[:, pl.ds(0, W)], {"tm": lax.rem(t + 1, T)}))
        lax.fori_loop(W + c * W, W + c * W + W, first_row, 0, unroll=2)

    flying = []
    for c in chunks:
        for cp in tms[c]:
            cp.wait_recv()
        transform(fwd_ref, tin, spec, c)
        rows, there_rows = pl.ds(c * W, W), pl.ds(W + c * W, W)
        copies = [remote(spec.at[rows, planes(lax.rem(s + k, S)), :], src.at[s, there_rows],
                         {"space": lax.rem(s + k, S)}) for k in range(1, S)]
        src[s, there_rows] = spec[rows, planes(s), :]
        if flying:
            land(*flying.pop())
        flying.append((c, copies))
    land(*flying.pop())
    for cp in halos:
        cp.wait_recv()
    lax.fori_loop(0, W, first_row, 0, unroll=2)
    lax.fori_loop(W + RB, R, first_row, 0, unroll=2)

    old, new = f0, f1
    solved = []
    for sweep in range(1, SWEEPS + 1):
        def sweep_row(r, c):
            mids = [old[x, r] for x in range(S)]
            for x in range(S):
                co = lambda i: sol_c[i, x, pl.ds(r + PAD - W, 1), :]
                total = src[x, r] + co(2) * old[x, r + 1] + co(3) * old[x, r - 1]
                total = total + co(4) * pltpu.roll(mids[x], NZ - 1, 1) + co(5) * pltpu.roll(mids[x], 1, 1)
                if x + 1 < S:
                    total = total + co(0) * mids[x + 1]
                if x > 0:
                    total = total + co(1) * mids[x - 1]
                update(x, r, total, new)
            return c

        if sweep < SWEEPS:
            lax.fori_loop(sweep, R - sweep, sweep_row, 0, unroll=2)
        else:
            for c in range(C):
                lax.fori_loop(W + c * W, W + c * W + W, sweep_row, 0, unroll=2)
                rows, from_rows = pl.ds(c * W, W), pl.ds(W + c * W, W)
                solved.append([remote(new.at[lax.rem(s + k, S), from_rows], spec2.at[rows, planes(s), :],
                                      {"space": lax.rem(s + k, S)}) for k in range(1, S)])
                spec2[rows, planes(s), :] = new[s, from_rows]
        old, new = new, old

    final = []
    for c in range(C):
        for cp in solved[c]:
            cp.wait_recv()
        transform(back_ref, spec2, outb, c)
        rows, home = pl.ds(c * W, W), pl.ds(RB * t + c * W, W)
        for k in range(1, T):
            to = lax.rem(t + k, T)
            final.append(remote(outb.at[rows, pl.ds(mult(N * to, 8), N), :], cor_ref.at[home], {"tm": to}))
        cor_ref[home] = outb[rows, pl.ds(mult(N * t, 8), N), :]
    for cp in final:
        cp.wait_recv()
    for cp in sent:
        cp.wait_send()


def local(T, S, iterate, forcing, start_field, classes, open_mask, diffusivity, drift):
    N, _, NY, NZ = iterate.shape
    L = N * T
    RB, Q = NY // T, T // S
    XB, G = Q * RB, L // S
    H, W = G // 2, SWEEPS
    R = RB + 2 * W
    fwd, back, shifts = step_tables(L, S)
    shifts = np.ascontiguousarray(np.broadcast_to(shifts, (3, L // 2, NZ)))
    C = RB // W
    copies = 2 * (S - 1) + 1 + 2 * C * Q * (S - 1) + 2 * C * (S - 1) + 2 + 2 * C * (T - 1)
    f32 = jnp.float32
    vmem = lambda *shape: pltpu.VMEM(shape, f32)
    VM, SM = pl.BlockSpec(memory_space=pltpu.VMEM), pl.BlockSpec(memory_space=pltpu.SMEM)
    ANY = pl.BlockSpec(memory_space=pl.ANY)
    res, cor = pl.pallas_call(
        functools.partial(kernel, T, S),
        out_shape=[jax.ShapeDtypeStruct((NY, N, NZ), f32)] * 2,
        in_specs=[ANY, ANY, VM, VM, VM, SM, SM, VM, VM, VM],
        out_specs=[VM, VM],
        scratch_shapes=[
            vmem(NY, N, NZ), vmem(NY, N, NZ), pltpu.SemaphoreType.DMA((2 * N,)),
            pltpu.VMEM((2, NY + 2 * PAD, NZ), jnp.int32), vmem(NY + 2, N, NZ), vmem(NY, NZ), vmem(NY, NZ),
            pltpu.VMEM((S, 2, XB, NZ), jnp.int32), pltpu.VMEM((S, 2, RB + 2 * PAD, NZ), jnp.int32),
            vmem(S, XB, NZ), vmem(S, XB, NZ), vmem(S, XB, N, NZ), vmem(S, XB, N, NZ), vmem(NY, N, NZ),
            vmem(6, NY, NZ), vmem(RB, L, NZ), vmem(RB, L, NZ),
            vmem(S, R, G, NZ), vmem(S, R, G, NZ), vmem(S, R, G, NZ),
            vmem(8, S, RB + 2 * PAD, NZ), vmem(3, S, R, H, NZ), vmem(RB, L, NZ), vmem(RB, L, NZ),
            pltpu.SemaphoreType.DMA((copies,)), pltpu.SemaphoreType.DMA((copies,)),
        ],
        compiler_params=pltpu.CompilerParams(collective_id=0, has_side_effects=True, vmem_limit_bytes=48 * 2**20),
        name="all_at_once",
    )(iterate[:, 0], forcing[:, 0], start_field[0], classes[0], open_mask[0], diffusivity, drift, fwd, back, shifts)
    return jnp.swapaxes(res, 0, 1)[:, None], jnp.swapaxes(cor, 0, 1)[:, None]


def solution(mesh):
    field, cells = P("tm", "space", None, None), P("space", None, None)
    return jax.shard_map(
        functools.partial(local, mesh.shape["tm"], mesh.shape["space"]),
        mesh=mesh,
        in_specs=(field, field, cells, cells, cells, P(), P()),
        out_specs=(field, field),
        check_vma=False,
    )
```

```python
import functools
import math

import jax
import jax.numpy as jnp
import ml_dtypes
import numpy as np
from jax import lax
from jax.experimental import pallas as pl
from jax.experimental.pallas import tpu as pltpu
from jax.sharding import PartitionSpec as P

SWEEPS = 4
ALPHA = 0.1
PAD = 8
MESH = pl.DeviceIdType.MESH


def step_tables(length, shares):
    half = length // 2
    planes = length // shares
    own = planes // 2
    index = np.arange(length)
    ramp = ALPHA ** (index / length)
    freq = np.arange(half)
    angle = 2.0 * math.pi * ((freq[:, None] * index[None, :]) % length) / length
    other = np.cos(math.pi * index)
    f_re, f_im = np.cos(angle), -np.sin(angle)
    f_im[0] = other
    scale = np.where(freq == 0, 1.0, 2.0)[:, None]
    b_re, b_im = scale * f_re, scale * f_im
    order = lambda re, im: np.stack([re.reshape(shares, own, -1), im.reshape(shares, own, -1)], 1).reshape(length, -1)
    forward = order(f_re, f_im) * ramp[None, :]
    back = (order(b_re, b_im) / (ramp[None, :] * length)).T
    root = ALPHA ** (1.0 / length)
    base = 2.0 * math.pi * freq / length
    re = 1.0 - root * np.cos(base)
    second = re.copy()
    second[0] = 1.0 + root
    im = root * np.sin(base)
    shifts = np.stack([re, second, im])[:, :, None].astype(np.float32)
    return split_matrix(forward), split_matrix(back), shifts


def split_matrix(matrix):
    high = matrix.astype(ml_dtypes.bfloat16)
    low = (matrix - high.astype(np.float64)).astype(ml_dtypes.bfloat16)
    return np.concatenate([high, high, low], axis=1)


def kernel(T, S, it_ref, fc_ref, start_ref, cls_ref, open_ref, diff_ref, drift_ref, fwd_ref, back_ref, shift_ref,
           res_ref, cor_ref,
           cm_ref, masked, last, arrived, cA, cB, xe, xw, xin, xout, xc, own_c, tin, spec, src, f0, f1,
           sol_c, inv, spec2, outb, ssem, rsem):
    NY, N, NZ = it_ref.shape
    L = N * T
    RB, Q = NY // T, T // S
    XB = Q * RB
    G = L // S
    H = G // 2
    W = SWEEPS
    R = RB + 2 * W
    C = RB // W
    chunks = [0, C - 1][:C] + list(range(1, C - 1))
    t, s = lax.axis_index("tm"), lax.axis_index("space")

    barrier = pltpu.get_barrier_semaphore()
    for k in range(1, S):
        pl.semaphore_signal(barrier, inc=1, device_id={"space": lax.rem(s + k, S)}, device_id_type=MESH)
    for k in range(1, T):
        pl.semaphore_signal(barrier, inc=1, device_id={"tm": lax.rem(t + k, T)}, device_id_type=MESH)

    used = [0]
    sent = []

    def remote(a, b, where):
        at = used[0]
        used[0] += 1
        copy = pltpu.make_async_remote_copy(src_ref=a, dst_ref=b, send_sem=ssem.at[at], recv_sem=rsem.at[at],
                                            device_id=where, device_id_type=MESH)
        copy.start()
        sent.append(copy)
        return copy

    def table(cls, ref_row):
        out = jnp.zeros(cls.shape, jnp.float32)
        for level in range(diff_ref.shape[0]):
            out = jnp.where(cls == level, ref_row(level), out)
        return out

    def mult(v, m):
        return pl.multiple_of(v, m)

    lane = lax.broadcasted_iota(jnp.int32, (1, NZ), 1)
    not_top = jnp.where(lane < NZ - 1, 1.0, 0.0)
    not_low = jnp.where(lane > 0, 1.0, 0.0)

    edge = jnp.zeros((PAD, NZ), jnp.int32)
    for i, ref in enumerate((cls_ref, open_ref)):
        cm_ref[i, 0:PAD, :] = edge
        cm_ref[i, PAD + NY:, :] = edge
        cm_ref[i, PAD:PAD + NY, :] = ref[...]
    cls = cls_ref[...]
    own_c[0] = open_ref[...].astype(jnp.float32)
    kappa = table(cls, lambda i: diff_ref[i])
    fy = kappa * table(cls, lambda i: drift_ref[1, i])
    fz = kappa * table(cls, lambda i: drift_ref[2, i])
    own_c[1] = 6.0 * kappa
    own_c[2] = kappa - fy
    own_c[3] = kappa + fy
    own_c[4] = (kappa - fz) * not_top
    own_c[5] = (kappa + fz) * not_low
    zero = jnp.zeros((N, NZ), jnp.float32)
    masked[0] = zero
    masked[NY + 1] = zero

    def mask_row(r, c):
        masked[r + 1] = it_ref[r] * own_c[0, pl.ds(r, 1), :]
        return c

    lax.fori_loop(0, NY, mask_row, 0, unroll=8)

    last[...] = it_ref[:, N - 1, :]
    pl.semaphore_wait(barrier, S - 1 + T - 1)

    cpA = [remote(cm_ref.at[:, pl.ds(mult(lax.rem(s + k, S) * XB + PAD, 8), XB)], cA.at[s],
                  {"space": lax.rem(s + k, S)}) for k in range(1, S)]
    pieces = [(c, jj) for c in chunks for jj in range(Q)]
    there = []

    def send_piece(c, jj):
        j = lax.rem(t + jj, Q)
        there.append([remote(masked.at[pl.ds((Q * lax.rem(s + k, S) + j) * RB + c * W + 1, W)],
                             xin.at[s, pl.ds(jj * RB + c * W, W)], {"space": lax.rem(s + k, S)}) for k in range(1, S)])
        xin[s, pl.ds(jj * RB + c * W, W)] = masked[pl.ds((Q * s + j) * RB + c * W + 1, W)]

    ahead, lag = 4, 2
    for piece in pieces[:ahead]:
        send_piece(*piece)
    cpL = remote(last, arrived, {"tm": lax.rem(t + 1, T)})
    cpB = [remote(cm_ref.at[:, pl.ds(mult(RB * t, 8), RB + 2 * PAD)], cB.at[s], {"space": lax.rem(s + k, S)})
           for k in range(1, S)]

    cA[s] = cm_ref[:, pl.ds(mult(s * XB + PAD, 8), XB), :]
    cB[s] = cm_ref[:, pl.ds(mult(RB * t, 8), RB + 2 * PAD), :]
    for cp in cpA:
        cp.wait_recv()

    def x_coefficients(x, c):
        cls = cA[x, 0]
        kappa = table(cls, lambda i: diff_ref[i])
        fx = kappa * table(cls, lambda i: drift_ref[0, i])
        xe[x] = kappa - fx
        xw[x] = kappa + fx
        return c

    lax.fori_loop(0, S, x_coefficients, 0)

    backs = []

    def couple_piece(c, jj, copies):
        j = lax.rem(t + jj, Q)
        for cp in copies:
            cp.wait_recv()
        base = jj * RB + c * W
        for r in range(W):
            row = j * RB + c * W + r
            fields = [xin[x, base + r] for x in range(S)]
            for x in range(S):
                total = None
                if x + 1 < S:
                    total = xe[x, pl.ds(row, 1), :] * fields[x + 1]
                if x > 0:
                    term = xw[x, pl.ds(row, 1), :] * fields[x - 1]
                    total = term if total is None else total + term
                xout[x, base + r] = zero if total is None else total
        home = pl.ds((Q * s + j) * RB + c * W, W)
        backs.append([remote(xout.at[lax.rem(s + k, S), pl.ds(base, W)], xc.at[home], {"space": lax.rem(s + k, S)})
                      for k in range(1, S)])
        xc[home] = xout[s, pl.ds(base, W)]

    first = lax.broadcasted_iota(jnp.int32, (N, NZ), 0) == 0

    def residual_row(r):
        it = it_ref[r]
        mk = masked[r + 1]
        co = lambda i: own_c[i, pl.ds(r, 1), :]
        previous = jnp.where(first, arrived[pl.ds(r, 1), :], pltpu.roll(it, 1, 0))
        cpl = co(2) * masked[r + 2] + co(3) * masked[r] + xc[r]
        cpl = cpl + co(4) * pltpu.roll(mk, NZ - 1, 1) + co(5) * pltpu.roll(mk, 1, 1)
        return co(0) * ((fc_ref[r] + previous - it) - (co(1) * mk - cpl))

    tms = {c: [] for c in chunks}

    def residual_piece(c, jj, copies):
        for cp in copies:
            cp.wait_recv()
        for m in list(range(1, S)) + [0]:
            k = jj + Q * m
            to = lax.rem(t + k, T)
            at = to * RB + c * W
            for r in range(W):
                res_ref[at + r] = residual_row(at + r)
            here = tin.at[pl.ds(c * W, W), pl.ds(mult(N * t, 8), N), :]
            if k:
                tms[c].append(remote(res_ref.at[pl.ds(at, W)], here, {"tm": to}))
            else:
                here[...] = res_ref[pl.ds(at, W)]

    for i in range(len(pieces) + lag):
        if i < len(pieces):
            couple_piece(*pieces[i], there[i])
        if i + ahead < len(pieces):
            send_piece(*pieces[i + ahead])
        if i == lag - 1:
            cpL.wait_recv()
            arrived[...] = jnp.where(t == 0, start_ref[...], arrived[...])
        if i >= lag:
            residual_piece(*pieces[i - lag], backs[i - lag])

    for cp in cpB:
        cp.wait_recv()

    def solve_coefficients(x, c):
        cls = cB[x, 0]
        kappa = table(cls, lambda i: diff_ref[i])
        fx = kappa * table(cls, lambda i: drift_ref[0, i])
        fy = kappa * table(cls, lambda i: drift_ref[1, i])
        fz = kappa * table(cls, lambda i: drift_ref[2, i])
        sol_c[0, x] = kappa - fx
        sol_c[1, x] = kappa + fx
        sol_c[2, x] = kappa - fy
        sol_c[3, x] = kappa + fy
        sol_c[4, x] = (kappa - fz) * not_top
        sol_c[5, x] = (kappa + fz) * not_low
        sol_c[6, x] = cB[x, 1].astype(jnp.float32)
        sol_c[7, x] = 6.0 * kappa
        return c

    lax.fori_loop(0, S, solve_coefficients, 0)
    own = pl.ds(mult(s * H, 8) if H % 8 == 0 else s * H, H)
    sh_re, sh_second, sh_im = shift_ref[0, own], shift_ref[1, own], shift_ref[2, own]

    def inverse_row(r, c):
        for x in range(S):
            k6 = sol_c[7, x, pl.ds(r + PAD - W, 1), :]
            w = sol_c[6, x, pl.ds(r + PAD - W, 1), :]
            a, b = sh_re + k6, sh_second + k6
            na = w / (a * a + sh_im * sh_im)
            nb = w / (b * b + sh_im * sh_im)
            inv[0, x, r] = a * na
            inv[1, x, r] = -sh_im * na
            inv[2, x, r] = b * nb
        return c

    lax.fori_loop(0, R, inverse_row, 0)

    def transform(matrix_ref, a, b, c):
        wide = jnp.concatenate([a[c * W + i] for i in range(W)], axis=1)
        high = wide.astype(jnp.bfloat16)
        low = (wide - high.astype(jnp.float32)).astype(jnp.bfloat16)
        wide = jnp.dot(matrix_ref[...], jnp.concatenate([high, low, high], axis=0), preferred_element_type=jnp.float32)
        for i in range(W):
            b[c * W + i] = wide[:, i * NZ:(i + 1) * NZ]

    def planes(who):
        return pl.ds(mult(G * who, 8), G)

    def update(x, r, total, out):
        re, im = total[:H], total[H:]
        a, b, d = inv[0, x, r], inv[1, x, r], inv[2, x, r]
        out[x, r] = jnp.concatenate([re * a - im * b, re * b + im * d], axis=0)

    def first_row(r, c):
        for x in range(S):
            update(x, r, src[x, r], f0)
        return c

    halos = []

    def land(c, copies):
        for cp in copies:
            cp.wait_recv()
        if c == 0:
            halos.append(remote(src.at[:, pl.ds(W, W)], src.at[:, pl.ds(RB + W, W)], {"tm": lax.rem(t + T - 1, T)}))
        if c == C - 1:
            halos.append(remote(src.at[:, pl.ds(RB, W)], src.at[:, pl.ds(0, W)], {"tm": lax.rem(t + 1, T)}))
        lax.fori_loop(W + c * W, W + c * W + W, first_row, 0, unroll=2)

    flying = []
    for c in chunks:
        for cp in tms[c]:
            cp.wait_recv()
        transform(fwd_ref, tin, spec, c)
        rows, there_rows = pl.ds(c * W, W), pl.ds(W + c * W, W)
        copies = [remote(spec.at[rows, planes(lax.rem(s + k, S)), :], src.at[s, there_rows],
                         {"space": lax.rem(s + k, S)}) for k in range(1, S)]
        src[s, there_rows] = spec[rows, planes(s), :]
        if flying:
            land(*flying.pop())
        flying.append((c, copies))
    land(*flying.pop())
    for cp in halos:
        cp.wait_recv()
    lax.fori_loop(0, W, first_row, 0, unroll=2)
    lax.fori_loop(W + RB, R, first_row, 0, unroll=2)

    old, new = f0, f1
    solved = []
    for sweep in range(1, SWEEPS + 1):
        def sweep_row(r, c):
            mids = [old[x, r] for x in range(S)]
            for x in range(S):
                co = lambda i: sol_c[i, x, pl.ds(r + PAD - W, 1), :]
                total = src[x, r] + co(2) * old[x, r + 1] + co(3) * old[x, r - 1]
                total = total + co(4) * pltpu.roll(mids[x], NZ - 1, 1) + co(5) * pltpu.roll(mids[x], 1, 1)
                if x + 1 < S:
                    total = total + co(0) * mids[x + 1]
                if x > 0:
                    total = total + co(1) * mids[x - 1]
                update(x, r, total, new)
            return c

        if sweep < SWEEPS:
            lax.fori_loop(sweep, R - sweep, sweep_row, 0, unroll=2)
        else:
            for c in range(C):
                lax.fori_loop(W + c * W, W + c * W + W, sweep_row, 0, unroll=2)
                rows, from_rows = pl.ds(c * W, W), pl.ds(W + c * W, W)
                solved.append([remote(new.at[lax.rem(s + k, S), from_rows], spec2.at[rows, planes(s), :],
                                      {"space": lax.rem(s + k, S)}) for k in range(1, S)])
                spec2[rows, planes(s), :] = new[s, from_rows]
        old, new = new, old

    final = []
    for c in range(C):
        for cp in solved[c]:
            cp.wait_recv()
        transform(back_ref, spec2, outb, c)
        rows, home = pl.ds(c * W, W), pl.ds(RB * t + c * W, W)
        for k in range(1, T):
            to = lax.rem(t + k, T)
            final.append(remote(outb.at[rows, pl.ds(mult(N * to, 8), N), :], cor_ref.at[home], {"tm": to}))
        cor_ref[home] = outb[rows, pl.ds(mult(N * t, 8), N), :]
    for cp in final:
        cp.wait_recv()
    for cp in sent:
        cp.wait_send()


def local(T, S, iterate, forcing, start_field, classes, open_mask, diffusivity, drift):
    N, _, NY, NZ = iterate.shape
    L = N * T
    RB, Q = NY // T, T // S
    XB, G = Q * RB, L // S
    H, W = G // 2, SWEEPS
    R = RB + 2 * W
    fwd, back, shifts = step_tables(L, S)
    it = jnp.swapaxes(iterate[:, 0], 0, 1)
    fc = jnp.swapaxes(forcing[:, 0], 0, 1)
    shifts = np.ascontiguousarray(np.broadcast_to(shifts, (3, L // 2, NZ)))
    C = RB // W
    copies = 2 * (S - 1) + 1 + 2 * C * Q * (S - 1) + 2 * C * (S - 1) + 2 + 2 * C * (T - 1)
    f32 = jnp.float32
    vmem = lambda *shape: pltpu.VMEM(shape, f32)
    VM, SM = pl.BlockSpec(memory_space=pltpu.VMEM), pl.BlockSpec(memory_space=pltpu.SMEM)
    res, cor = pl.pallas_call(
        functools.partial(kernel, T, S),
        out_shape=[jax.ShapeDtypeStruct((NY, N, NZ), f32)] * 2,
        in_specs=[VM, VM, VM, VM, VM, SM, SM, VM, VM, VM],
        out_specs=[VM, VM],
        scratch_shapes=[
            pltpu.VMEM((2, NY + 2 * PAD, NZ), jnp.int32), vmem(NY + 2, N, NZ), vmem(NY, NZ), vmem(NY, NZ),
            pltpu.VMEM((S, 2, XB, NZ), jnp.int32), pltpu.VMEM((S, 2, RB + 2 * PAD, NZ), jnp.int32),
            vmem(S, XB, NZ), vmem(S, XB, NZ), vmem(S, XB, N, NZ), vmem(S, XB, N, NZ), vmem(NY, N, NZ),
            vmem(6, NY, NZ), vmem(RB, L, NZ), vmem(RB, L, NZ),
            vmem(S, R, G, NZ), vmem(S, R, G, NZ), vmem(S, R, G, NZ),
            vmem(8, S, RB + 2 * PAD, NZ), vmem(3, S, R, H, NZ), vmem(RB, L, NZ), vmem(RB, L, NZ),
            pltpu.SemaphoreType.DMA((copies,)), pltpu.SemaphoreType.DMA((copies,)),
        ],
        compiler_params=pltpu.CompilerParams(collective_id=0, has_side_effects=True, vmem_limit_bytes=48 * 2**20),
        name="all_at_once",
    )(it, fc, start_field[0], classes[0], open_mask[0], diffusivity, drift, fwd, back, shifts)
    return jnp.swapaxes(res, 0, 1)[:, None], jnp.swapaxes(cor, 0, 1)[:, None]


def solution(mesh):
    field, cells = P("tm", "space", None, None), P("space", None, None)
    return jax.shard_map(
        functools.partial(local, mesh.shape["tm"], mesh.shape["space"]),
        mesh=mesh,
        in_specs=(field, field, cells, cells, cells, P(), P()),
        out_specs=(field, field),
        check_vma=False,
    )
```

```python
import functools
import math

import jax
import jax.numpy as jnp
import ml_dtypes
import numpy as np
from jax import lax
from jax.experimental import pallas as pl
from jax.experimental.pallas import tpu as pltpu
from jax.sharding import PartitionSpec as P

SWEEPS = 4
ALPHA = 0.1
PAD = 8
MESH = pl.DeviceIdType.MESH


def step_tables(length, shares):
    half = length // 2
    planes = length // shares
    own = planes // 2
    index = np.arange(length)
    ramp = ALPHA ** (index / length)
    freq = np.arange(half)
    angle = 2.0 * math.pi * ((freq[:, None] * index[None, :]) % length) / length
    other = np.cos(math.pi * index)
    f_re, f_im = np.cos(angle), -np.sin(angle)
    f_im[0] = other
    scale = np.where(freq == 0, 1.0, 2.0)[:, None]
    b_re, b_im = scale * f_re, scale * f_im
    order = lambda re, im: np.stack([re.reshape(shares, own, -1), im.reshape(shares, own, -1)], 1).reshape(length, -1)
    forward = order(f_re, f_im) * ramp[None, :]
    back = (order(b_re, b_im) / (ramp[None, :] * length)).T
    root = ALPHA ** (1.0 / length)
    base = 2.0 * math.pi * freq / length
    re = 1.0 - root * np.cos(base)
    second = re.copy()
    second[0] = 1.0 + root
    im = root * np.sin(base)
    shifts = np.stack([re, second, im])[:, :, None].astype(np.float32)
    return split_matrix(forward), split_matrix(back), shifts


def split_matrix(matrix):
    high = matrix.astype(ml_dtypes.bfloat16)
    low = (matrix - high.astype(np.float64)).astype(ml_dtypes.bfloat16)
    return np.concatenate([high, high, low], axis=1)


def kernel(T, S, it_ref, fc_ref, start_ref, cls_ref, open_ref, diff_ref, drift_ref, fwd_ref, back_ref, shift_ref,
           res_ref, cor_ref,
           cm_ref, masked, last, arrived, cA, cB, xe, xw, xin, xout, xc, own_c, tin, spec, src, f0, f1,
           sol_c, inv, spec2, outb, ssem, rsem):
    NY, N, NZ = it_ref.shape
    L = N * T
    RB, Q = NY // T, T // S
    XB = Q * RB
    G = L // S
    H = G // 2
    W = SWEEPS
    R = RB + 2 * W
    C = RB // W
    chunks = [0, C - 1][:C] + list(range(1, C - 1))
    t, s = lax.axis_index("tm"), lax.axis_index("space")

    barrier = pltpu.get_barrier_semaphore()
    for k in range(1, S):
        pl.semaphore_signal(barrier, inc=1, device_id={"space": lax.rem(s + k, S)}, device_id_type=MESH)
    for k in range(1, T):
        pl.semaphore_signal(barrier, inc=1, device_id={"tm": lax.rem(t + k, T)}, device_id_type=MESH)

    used = [0]
    sent = []

    def remote(a, b, where):
        at = used[0]
        used[0] += 1
        copy = pltpu.make_async_remote_copy(src_ref=a, dst_ref=b, send_sem=ssem.at[at], recv_sem=rsem.at[at],
                                            device_id=where, device_id_type=MESH)
        copy.start()
        sent.append(copy)
        return copy

    def table(cls, ref_row):
        out = jnp.zeros(cls.shape, jnp.float32)
        for level in range(diff_ref.shape[0]):
            out = jnp.where(cls == level, ref_row(level), out)
        return out

    def mult(v, m):
        return pl.multiple_of(v, m)

    lane = lax.broadcasted_iota(jnp.int32, (1, NZ), 1)
    not_top = jnp.where(lane < NZ - 1, 1.0, 0.0)
    not_low = jnp.where(lane > 0, 1.0, 0.0)

    edge = jnp.zeros((PAD, NZ), jnp.int32)
    for i, ref in enumerate((cls_ref, open_ref)):
        cm_ref[i, 0:PAD, :] = edge
        cm_ref[i, PAD + NY:, :] = edge
        cm_ref[i, PAD:PAD + NY, :] = ref[...]
    cls = cls_ref[...]
    own_c[0] = open_ref[...].astype(jnp.float32)
    kappa = table(cls, lambda i: diff_ref[i])
    fy = kappa * table(cls, lambda i: drift_ref[1, i])
    fz = kappa * table(cls, lambda i: drift_ref[2, i])
    own_c[1] = 6.0 * kappa
    own_c[2] = kappa - fy
    own_c[3] = kappa + fy
    own_c[4] = (kappa - fz) * not_top
    own_c[5] = (kappa + fz) * not_low
    zero = jnp.zeros((N, NZ), jnp.float32)
    masked[0] = zero
    masked[NY + 1] = zero

    def mask_row(r, c):
        masked[r + 1] = it_ref[r] * own_c[0, pl.ds(r, 1), :]
        return c

    lax.fori_loop(0, NY, mask_row, 0, unroll=8)

    last[...] = it_ref[:, N - 1, :]
    pl.semaphore_wait(barrier, S - 1 + T - 1)

    cpA = [remote(cm_ref.at[:, pl.ds(mult(lax.rem(s + k, S) * XB + PAD, 8), XB)], cA.at[s],
                  {"space": lax.rem(s + k, S)}) for k in range(1, S)]
    pieces = [(c, jj) for c in chunks for jj in range(Q)]
    there = []

    def send_piece(c, jj):
        j = lax.rem(t + jj, Q)
        there.append([remote(masked.at[pl.ds((Q * lax.rem(s + k, S) + j) * RB + c * W + 1, W)],
                             xin.at[s, pl.ds(jj * RB + c * W, W)], {"space": lax.rem(s + k, S)}) for k in range(1, S)])
        xin[s, pl.ds(jj * RB + c * W, W)] = masked[pl.ds((Q * s + j) * RB + c * W + 1, W)]

    ahead, lag = 4, 1
    for piece in pieces[:ahead]:
        send_piece(*piece)
    cpL = remote(last, arrived, {"tm": lax.rem(t + 1, T)})
    cpB = [remote(cm_ref.at[:, pl.ds(mult(RB * t, 8), RB + 2 * PAD)], cB.at[s], {"space": lax.rem(s + k, S)})
           for k in range(1, S)]

    cA[s] = cm_ref[:, pl.ds(mult(s * XB + PAD, 8), XB), :]
    cB[s] = cm_ref[:, pl.ds(mult(RB * t, 8), RB + 2 * PAD), :]
    for cp in cpA:
        cp.wait_recv()

    def x_coefficients(x, c):
        cls = cA[x, 0]
        kappa = table(cls, lambda i: diff_ref[i])
        fx = kappa * table(cls, lambda i: drift_ref[0, i])
        xe[x] = kappa - fx
        xw[x] = kappa + fx
        return c

    lax.fori_loop(0, S, x_coefficients, 0)

    backs = []

    def couple_piece(c, jj, copies):
        j = lax.rem(t + jj, Q)
        for cp in copies:
            cp.wait_recv()
        base = jj * RB + c * W
        for r in range(W):
            row = j * RB + c * W + r
            fields = [xin[x, base + r] for x in range(S)]
            for x in range(S):
                total = None
                if x + 1 < S:
                    total = xe[x, pl.ds(row, 1), :] * fields[x + 1]
                if x > 0:
                    term = xw[x, pl.ds(row, 1), :] * fields[x - 1]
                    total = term if total is None else total + term
                xout[x, base + r] = zero if total is None else total
        home = pl.ds((Q * s + j) * RB + c * W, W)
        backs.append([remote(xout.at[lax.rem(s + k, S), pl.ds(base, W)], xc.at[home], {"space": lax.rem(s + k, S)})
                      for k in range(1, S)])
        xc[home] = xout[s, pl.ds(base, W)]

    first = lax.broadcasted_iota(jnp.int32, (N, NZ), 0) == 0

    def residual_row(r):
        it = it_ref[r]
        mk = masked[r + 1]
        co = lambda i: own_c[i, pl.ds(r, 1), :]
        previous = jnp.where(first, arrived[pl.ds(r, 1), :], pltpu.roll(it, 1, 0))
        cpl = co(2) * masked[r + 2] + co(3) * masked[r] + xc[r]
        cpl = cpl + co(4) * pltpu.roll(mk, NZ - 1, 1) + co(5) * pltpu.roll(mk, 1, 1)
        return co(0) * ((fc_ref[r] + previous - it) - (co(1) * mk - cpl))

    tms = {c: [] for c in chunks}

    def residual_piece(c, jj, copies):
        for cp in copies:
            cp.wait_recv()
        for m in list(range(1, S)) + [0]:
            k = jj + Q * m
            to = lax.rem(t + k, T)
            at = to * RB + c * W
            for r in range(W):
                res_ref[at + r] = residual_row(at + r)
            here = tin.at[pl.ds(c * W, W), pl.ds(mult(N * t, 8), N), :]
            if k:
                tms[c].append(remote(res_ref.at[pl.ds(at, W)], here, {"tm": to}))
            else:
                here[...] = res_ref[pl.ds(at, W)]

    for i in range(len(pieces) + lag):
        if i < len(pieces):
            couple_piece(*pieces[i], there[i])
        if i + ahead < len(pieces):
            send_piece(*pieces[i + ahead])
        if i == lag - 1:
            cpL.wait_recv()
            arrived[...] = jnp.where(t == 0, start_ref[...], arrived[...])
        if i >= lag:
            residual_piece(*pieces[i - lag], backs[i - lag])

    for cp in cpB:
        cp.wait_recv()

    def solve_coefficients(x, c):
        cls = cB[x, 0]
        kappa = table(cls, lambda i: diff_ref[i])
        fx = kappa * table(cls, lambda i: drift_ref[0, i])
        fy = kappa * table(cls, lambda i: drift_ref[1, i])
        fz = kappa * table(cls, lambda i: drift_ref[2, i])
        sol_c[0, x] = kappa - fx
        sol_c[1, x] = kappa + fx
        sol_c[2, x] = kappa - fy
        sol_c[3, x] = kappa + fy
        sol_c[4, x] = (kappa - fz) * not_top
        sol_c[5, x] = (kappa + fz) * not_low
        sol_c[6, x] = cB[x, 1].astype(jnp.float32)
        sol_c[7, x] = 6.0 * kappa
        return c

    lax.fori_loop(0, S, solve_coefficients, 0)
    own = pl.ds(mult(s * H, 8) if H % 8 == 0 else s * H, H)
    sh_re, sh_second, sh_im = shift_ref[0, own], shift_ref[1, own], shift_ref[2, own]

    def inverse_row(r, c):
        for x in range(S):
            k6 = sol_c[7, x, pl.ds(r + PAD - W, 1), :]
            w = sol_c[6, x, pl.ds(r + PAD - W, 1), :]
            a, b = sh_re + k6, sh_second + k6
            na = w / (a * a + sh_im * sh_im)
            nb = w / (b * b + sh_im * sh_im)
            inv[0, x, r] = a * na
            inv[1, x, r] = -sh_im * na
            inv[2, x, r] = b * nb
        return c

    lax.fori_loop(0, R, inverse_row, 0)

    def transform(matrix_ref, a, b, c):
        wide = jnp.concatenate([a[c * W + i] for i in range(W)], axis=1)
        high = wide.astype(jnp.bfloat16)
        low = (wide - high.astype(jnp.float32)).astype(jnp.bfloat16)
        wide = jnp.dot(matrix_ref[...], jnp.concatenate([high, low, high], axis=0), preferred_element_type=jnp.float32)
        for i in range(W):
            b[c * W + i] = wide[:, i * NZ:(i + 1) * NZ]

    def planes(who):
        return pl.ds(mult(G * who, 8), G)

    def update(x, r, total, out):
        re, im = total[:H], total[H:]
        a, b, d = inv[0, x, r], inv[1, x, r], inv[2, x, r]
        out[x, r] = jnp.concatenate([re * a - im * b, re * b + im * d], axis=0)

    def first_row(r, c):
        for x in range(S):
            update(x, r, src[x, r], f0)
        return c

    halos = []

    def land(c, copies):
        for cp in copies:
            cp.wait_recv()
        if c == 0:
            halos.append(remote(src.at[:, pl.ds(W, W)], src.at[:, pl.ds(RB + W, W)], {"tm": lax.rem(t + T - 1, T)}))
        if c == C - 1:
            halos.append(remote(src.at[:, pl.ds(RB, W)], src.at[:, pl.ds(0, W)], {"tm": lax.rem(t + 1, T)}))
        lax.fori_loop(W + c * W, W + c * W + W, first_row, 0, unroll=4)

    flying = []
    for c in chunks:
        for cp in tms[c]:
            cp.wait_recv()
        transform(fwd_ref, tin, spec, c)
        rows, there_rows = pl.ds(c * W, W), pl.ds(W + c * W, W)
        copies = [remote(spec.at[rows, planes(lax.rem(s + k, S)), :], src.at[s, there_rows],
                         {"space": lax.rem(s + k, S)}) for k in range(1, S)]
        src[s, there_rows] = spec[rows, planes(s), :]
        if flying:
            land(*flying.pop())
        flying.append((c, copies))
    land(*flying.pop())
    for cp in halos:
        cp.wait_recv()
    lax.fori_loop(0, W, first_row, 0, unroll=2)
    lax.fori_loop(W + RB, R, first_row, 0, unroll=2)

    old, new = f0, f1
    solved = []
    for sweep in range(1, SWEEPS + 1):
        def sweep_row(r, c):
            mids = [old[x, r] for x in range(S)]
            for x in range(S):
                co = lambda i: sol_c[i, x, pl.ds(r + PAD - W, 1), :]
                total = src[x, r] + co(2) * old[x, r + 1] + co(3) * old[x, r - 1]
                total = total + co(4) * pltpu.roll(mids[x], NZ - 1, 1) + co(5) * pltpu.roll(mids[x], 1, 1)
                if x + 1 < S:
                    total = total + co(0) * mids[x + 1]
                if x > 0:
                    total = total + co(1) * mids[x - 1]
                update(x, r, total, new)
            return c

        if sweep < SWEEPS:
            lax.fori_loop(sweep, R - sweep, sweep_row, 0, unroll=2)
        else:
            for c in range(C):
                lax.fori_loop(W + c * W, W + c * W + W, sweep_row, 0, unroll=4)
                rows, from_rows = pl.ds(c * W, W), pl.ds(W + c * W, W)
                solved.append([remote(new.at[lax.rem(s + k, S), from_rows], spec2.at[rows, planes(s), :],
                                      {"space": lax.rem(s + k, S)}) for k in range(1, S)])
                spec2[rows, planes(s), :] = new[s, from_rows]
        old, new = new, old

    final = []
    for c in range(C):
        for cp in solved[c]:
            cp.wait_recv()
        transform(back_ref, spec2, outb, c)
        rows, home = pl.ds(c * W, W), pl.ds(RB * t + c * W, W)
        for k in range(1, T):
            to = lax.rem(t + k, T)
            final.append(remote(outb.at[rows, pl.ds(mult(N * to, 8), N), :], cor_ref.at[home], {"tm": to}))
        cor_ref[home] = outb[rows, pl.ds(mult(N * t, 8), N), :]
    for cp in final:
        cp.wait_recv()
    for cp in sent:
        cp.wait_send()


def local(T, S, iterate, forcing, start_field, classes, open_mask, diffusivity, drift):
    N, _, NY, NZ = iterate.shape
    L = N * T
    RB, Q = NY // T, T // S
    XB, G = Q * RB, L // S
    H, W = G // 2, SWEEPS
    R = RB + 2 * W
    fwd, back, shifts = step_tables(L, S)
    it = jnp.swapaxes(iterate[:, 0], 0, 1)
    fc = jnp.swapaxes(forcing[:, 0], 0, 1)
    shifts = np.ascontiguousarray(np.broadcast_to(shifts, (3, L // 2, NZ)))
    C = RB // W
    copies = 2 * (S - 1) + 1 + 2 * C * Q * (S - 1) + 2 * C * (S - 1) + 2 + 2 * C * (T - 1)
    f32 = jnp.float32
    vmem = lambda *shape: pltpu.VMEM(shape, f32)
    VM, SM = pl.BlockSpec(memory_space=pltpu.VMEM), pl.BlockSpec(memory_space=pltpu.SMEM)
    res, cor = pl.pallas_call(
        functools.partial(kernel, T, S),
        out_shape=[jax.ShapeDtypeStruct((NY, N, NZ), f32)] * 2,
        in_specs=[VM, VM, VM, VM, VM, SM, SM, VM, VM, VM],
        out_specs=[VM, VM],
        scratch_shapes=[
            pltpu.VMEM((2, NY + 2 * PAD, NZ), jnp.int32), vmem(NY + 2, N, NZ), vmem(NY, NZ), vmem(NY, NZ),
            pltpu.VMEM((S, 2, XB, NZ), jnp.int32), pltpu.VMEM((S, 2, RB + 2 * PAD, NZ), jnp.int32),
            vmem(S, XB, NZ), vmem(S, XB, NZ), vmem(S, XB, N, NZ), vmem(S, XB, N, NZ), vmem(NY, N, NZ),
            vmem(6, NY, NZ), vmem(RB, L, NZ), vmem(RB, L, NZ),
            vmem(S, R, G, NZ), vmem(S, R, G, NZ), vmem(S, R, G, NZ),
            vmem(8, S, RB + 2 * PAD, NZ), vmem(3, S, R, H, NZ), vmem(RB, L, NZ), vmem(RB, L, NZ),
            pltpu.SemaphoreType.DMA((copies,)), pltpu.SemaphoreType.DMA((copies,)),
        ],
        compiler_params=pltpu.CompilerParams(collective_id=0, has_side_effects=True, vmem_limit_bytes=48 * 2**20),
        name="all_at_once",
    )(it, fc, start_field[0], classes[0], open_mask[0], diffusivity, drift, fwd, back, shifts)
    return jnp.swapaxes(res, 0, 1)[:, None], jnp.swapaxes(cor, 0, 1)[:, None]


def solution(mesh):
    field, cells = P("tm", "space", None, None), P("space", None, None)
    return jax.shard_map(
        functools.partial(local, mesh.shape["tm"], mesh.shape["space"]),
        mesh=mesh,
        in_specs=(field, field, cells, cells, cells, P(), P()),
        out_specs=(field, field),
        check_vma=False,
    )
```
